32 devices in a mesh: section: 4 (over y, x), tile: 8 (over z, core).
Axes of the slice: x: 2, y: 2, z: 4, core: 2. Of those that a mesh axis runs over, the one named last changes fastest.
Arguments:
- carried_act: bfloat16 [4, 48, 16, 16, 256], P('section', 'tile'), may hold values from -6 to 6
- stored_out: bfloat16 [4, 48, 16, 16, 256], P('section', 'tile'), may hold values from -6 to 6
- cotangent: bfloat16 [4, 48, 16, 16, 256], P('section', 'tile'), may hold values from -6 to 6
- weights: bfloat16 [4, 2, 27, 128, 128], P('section'), may hold values from -0.109375 to 0.109375
- momentum: float32 [4, 2, 27, 128, 128], P('section'), may hold values from -6 to 6
Outputs:
- forward_out: bfloat16 [4, 48, 16, 16, 256], P('section', 'tile')
- input_grad: bfloat16 [4, 48, 16, 16, 256], P('section', 'tile')
- new_momentum: float32 [4, 2, 27, 128, 128], P('section')
The draws below stay inside these ranges and needn't reach their ends.
All inputs are finite; a program needn't handle non-finite values.
Results may differ from the reference program's by a relative error of at most 0.006.
Values may be sent and summed in bfloat16 or wider, within the bound.
A program may use at most 128 MiB of HBM per device.

```python
import jax
import jax.numpy as jnp
from jax import lax

HALF = 128
HY = 16
WX = 16
SECTIONS = 4
NZ = 48


def block_scale(own_key, dims, split, low, high):
    loudness, own = 1.0, jax.random.fold_in(own_key, 6)
    for axis_at, parts in split:
        draws = jnp.exp(jax.random.uniform(jax.random.fold_in(own, axis_at), (parts,), jnp.float32, low / len(split), high / len(split)))
        loudness = loudness * jnp.repeat(draws, dims[axis_at] // parts).reshape([-1 if axis == axis_at else 1 for axis in range(len(dims))])
    return loudness


def bell_draw(key, shape, spread, reach, split=(), dtype=jnp.bfloat16):
    loudness = block_scale(key, shape, split, -0.22, 0.18) if split else 1.0
    array = jax.random.normal(key, shape, jnp.float32) * spread * loudness
    return jnp.minimum(jnp.maximum(array, -reach), reach).astype(dtype)


def setup_inputs(seed: int = 0) -> dict:
    key_list = jax.random.split(jax.random.key(seed), 6)
    carried_act = bell_draw(key_list[0], (SECTIONS, NZ, HY, WX, 2 * HALF), 1.0, 6.0, ((0, 4), (1, 8)))
    stored_out = bell_draw(key_list[1], (SECTIONS, NZ, HY, WX, 2 * HALF), 1.0, 6.0, ((0, 4), (1, 8)))
    cotangent = bell_draw(key_list[2], (SECTIONS, NZ, HY, WX, 2 * HALF), 1.0, 6.0, ((0, 4), (1, 8)))
    weights = bell_draw(key_list[3], (SECTIONS, 2, 27, HALF, HALF), (27 * HALF) ** -0.5, 0.109375, ((0, 4),))
    momentum = bell_draw(key_list[4], (SECTIONS, 2, 27, HALF, HALF), 1.0, 6.0, ((0, 4),), jnp.float32)
    return dict(carried_act=carried_act, stored_out=stored_out, cotangent=cotangent, weights=weights, momentum=momentum)


momentum_decay = 0.9
grad_weight = 0.25

def flatten(field):
    return field.reshape(-1, field.shape[-1])

def columns(padded, depth, rows, cols):
    pieces = []
    for i in range(3):
        for j in range(3):
            for k in range(3):
                pieces.append(padded[i:i + depth, j:j + rows, k:k + cols, :])
    return flatten(jnp.concatenate(pieces, axis=-1))

def unfold(field):
    depth, rows, cols, chans = field.shape
    padded = jnp.pad(field, ((1, 1), (1, 1), (1, 1), (0, 0)))
    return columns(padded, depth, rows, cols)

def convolve(unfolded, weight):
    return jnp.dot(unfolded, weight.reshape(-1, weight.shape[-1]), preferred_element_type=jnp.float32)

def flipped(weight):
    return jnp.transpose(jnp.flip(weight, 0), (0, 2, 1))

def section_step(fwd_in, stored, coming, weight):
    half = weight.shape[-1]
    shape = fwd_in.shape[:3] + (half,)
    w_f = weight[0]
    w_g = weight[1]
    a_one = fwd_in[..., :half]
    a_two = fwd_in[..., half:]
    f_val = jnp.tanh(convolve(unfold(a_two), w_f)).reshape(shape)
    b_one = (a_one.astype(jnp.float32) + f_val).astype(jnp.bfloat16)
    g_val = jnp.tanh(convolve(unfold(b_one), w_g)).reshape(shape)
    b_two = (a_two.astype(jnp.float32) + g_val).astype(jnp.bfloat16)
    out_fwd = jnp.concatenate([b_one, b_two], axis=-1)
    z_one = stored[..., :half]
    z_two = stored[..., half:]
    c_one = coming[..., :half]
    c_two = coming[..., half:]
    cols_z = unfold(z_one)
    g_rec = jnp.tanh(convolve(cols_z, w_g)).reshape(shape)
    r_two = (z_two.astype(jnp.float32) - g_rec).astype(jnp.bfloat16)
    cols_r = unfold(r_two)
    f_rec = jnp.tanh(convolve(cols_r, w_f)).reshape(shape)
    pre_g = (c_two.astype(jnp.float32) * (1.0 - g_rec * g_rec)).astype(jnp.bfloat16)
    d_one = (c_one.astype(jnp.float32) + convolve(unfold(pre_g), flipped(w_g)).reshape(shape)).astype(jnp.bfloat16)
    pre_f = (d_one.astype(jnp.float32) * (1.0 - f_rec * f_rec)).astype(jnp.bfloat16)
    d_two = (c_two.astype(jnp.float32) + convolve(unfold(pre_f), flipped(w_f)).reshape(shape)).astype(jnp.bfloat16)
    out_grad = jnp.concatenate([d_one, d_two], axis=-1)
    grad_f = jnp.dot(cols_r.T, flatten(pre_f), preferred_element_type=jnp.float32)
    grad_g = jnp.dot(cols_z.T, flatten(pre_g), preferred_element_type=jnp.float32)
    grads = jnp.stack([grad_f, grad_g]).reshape(weight.shape)
    return (out_fwd, out_grad, grads)

def reference(carried_act, stored_out, cotangent, weights, momentum):
    fwd_in = jnp.roll(carried_act, 1, axis=0)
    coming = jnp.roll(cotangent, -1, axis=0)

    def one(items):
        return section_step(items[0], items[1], items[2], items[3])
    out_fwd, out_grad, grads = lax.map(one, (fwd_in, stored_out, coming, weights))
    total = NZ * HY * WX
    grads = grads * (grad_weight / jnp.sqrt(jnp.float32(total)))
    new_momentum = momentum_decay * momentum + grads
    return (out_fwd, out_grad, new_momentum)
```

```python
import functools

import jax
import jax.numpy as jnp
from jax import lax
from jax.experimental import pallas as pl
from jax.experimental.pallas import tpu as pltpu
from jax.sharding import PartitionSpec as P

momentum_decay = 0.9
grad_weight = 0.25
BF = jnp.bfloat16
F32 = jnp.float32


def kernel(
    ns, nt, tp, step,
    act, stored, cot, w,
    fwd, igrad, gsum,
    xz, xr, xpg, xpf, xa, xb, halo, a_in, c_in, gz_s, fz_s, wt, pg_s, pf_s,
    grad, got1, part, got2, total, send, recv,
):
    depth, hy, wx = a_in.shape[1:4]
    half = w.shape[-1]
    s = lax.axis_index("section")
    t = lax.axis_index("tile")
    m = nt // 2
    chip, core = t // 2, lax.rem(t, 2)
    partner = 2 * chip + (1 - core)
    nxt, prv = lax.rem(s + 1, ns), lax.rem(s + ns - 1, ns)
    has_low, has_high = t > 0, t < nt - 1
    plane = hy * wx
    rows = step * plane
    steps = depth // step
    used = [0]

    def at(sec, tile):
        return {"section": sec, "tile": tile}

    def copy(src, dst, sec, tile):
        i = used[0]
        used[0] += 1
        return pltpu.make_async_remote_copy(
            src_ref=src, dst_ref=dst, send_sem=send.at[i], recv_sem=recv.at[i],
            device_id=at(sec, tile), device_id_type=pl.DeviceIdType.MESH,
        )

    barrier = pltpu.get_barrier_semaphore()

    def hail(sec, tile):
        pl.semaphore_signal(
            barrier, inc=1, device_id=at(sec, tile), device_id_type=pl.DeviceIdType.MESH
        )

    hail(nxt, t)
    hail(prv, t)
    for d in range(1, m):
        hail(s, lax.rem(t + 2 * d, nt))

    hail(s, lax.rem(t + 1, nt))
    hail(s, lax.rem(t + nt - 1, nt))
    pl.semaphore_wait(barrier, m + 3)

    def mid(x, z):
        return x.at[z, pl.ds(1, hy), :, pl.ds(half, half)]

    def halo_copies(slot, first, last):
        down = copy(first, halo.at[slot, 1], s, lax.rem(t + nt - 1, nt))
        up = copy(last, halo.at[slot, 0], s, lax.rem(t + 1, nt))
        return down, up

    def halo_start(pair):
        @pl.when(has_low)
        def _():
            pair[0].start()

        @pl.when(has_high)
        def _():
            pair[1].start()

    def fill(x, z, count, value):
        n = count * plane
        value = value.reshape(n, half)
        col = lax.rem(lax.broadcasted_iota(jnp.int32, (n, half), 0), wx)
        left = jnp.where(col == 0, 0.0, pltpu.roll(value, 1, 0))
        right = jnp.where(col == wx - 1, 0.0, pltpu.roll(value, n - 1, 0))
        for k, v in enumerate((left, value, right)):
            x[pl.ds(z, count), pl.ds(1, hy), :, pl.ds(k * half, half)] = (
                v.astype(BF).reshape(count, hy, wx, half)
            )

    def halo_finish(pair, slot, x):
        @pl.when(has_low)
        def _():
            pair[0].wait_send()
            pair[1].wait_recv()
            fill(x, 0, 1, halo[slot, 0].astype(F32))

        @pl.when(has_high)
        def _():
            pair[1].wait_send()
            pair[0].wait_recv()
            fill(x, depth + 1, 1, halo[slot, 1].astype(F32))

    def clear(x):
        edge = jnp.zeros((depth + 2, 1, wx, 3 * half), BF)
        x[:, pl.ds(0, 1)] = edge
        x[:, pl.ds(hy + 1, 1)] = edge
        empty = jnp.zeros((1, hy, wx, 3 * half), BF)

        @pl.when(t == 0)
        def _():
            x[pl.ds(0, 1), pl.ds(1, hy)] = empty

        @pl.when(t == nt - 1)
        def _():
            x[pl.ds(depth + 1, 1), pl.ds(1, hy)] = empty

    def conv(x, weight, z):
        cols = jnp.concatenate(
            [
                x[pl.ds(z + i, step), pl.ds(j, hy)].reshape(rows, 3 * half)
                for i in range(3)
                for j in range(3)
            ],
            axis=1,
        )
        return jnp.dot(cols, weight, preferred_element_type=F32)

    def block(ref, z, part_at, *lead):
        return ref[(*lead, pl.ds(z, step), slice(None), slice(None), pl.ds(part_at * half, half))].astype(
            F32
        ).reshape(rows, half)

    def put(ref, z, part_at, value):
        ref[pl.ds(z, step), :, :, pl.ds(part_at * half, half)] = value.astype(BF).reshape(
            step, hy, wx, half
        )

    def each(body):
        def run(n, carry):
            body(n * step)
            return carry

        lax.fori_loop(0, steps, run, 0)

    z_halo = halo_copies(
        0, stored.at[0, 0, :, :, pl.ds(0, half)], stored.at[0, depth - 1, :, :, pl.ds(0, half)]
    )
    halo_start(z_halo)
    parts = {}
    for name, src, dst, target, piece in (
        ("c2", cot, c_in, prv, 1),
        ("c1", cot, c_in, prv, 0),
        ("a2", act, a_in, nxt, 1),
        ("a1", act, a_in, nxt, 0),
    ):
        view = (0, slice(None), slice(None), slice(None), pl.ds(piece * half, half))
        parts[name] = copy(src.at[view], dst.at[view], target, t)
        parts[name].start()

    for x in (xz, xr, xpg, xpf, xa, xb):
        clear(x)
    each(lambda z: fill(xz, z + 1, step, block(stored, z, 0, 0)))

    def turn(n, carry):
        for which in range(2):
            wt[which, n] = w[0, which, 26 - n].T
        return carry

    lax.fori_loop(0, 27, turn, 0)
    halo_finish(z_halo, 0, xz)

    def flat(ref, *lead):
        return ref[lead].reshape(27 * half, half)

    def reconstruct(z):
        g = jnp.tanh(conv(xz, flat(w, 0, 1), z))
        gz_s[pl.ds(z, step)] = (1.0 - g * g).reshape(step, plane, half)
        fill(xr, z + 1, step, block(stored, z, 1, 0) - g)

    each(reconstruct)
    r_halo = halo_copies(1, mid(xr, 1), mid(xr, depth))
    halo_start(r_halo)
    parts["c2"].wait()

    def pre_g(z):
        v = block(c_in, z, 1, 0) * gz_s[pl.ds(z, step)].reshape(rows, half)
        pg_s[pl.ds(z, step)] = v.astype(BF).reshape(step, plane, half)
        fill(xpg, z + 1, step, v)

    each(pre_g)
    pg_halo = halo_copies(2, mid(xpg, 1), mid(xpg, depth))
    halo_start(pg_halo)

    def wgrad(x, d_ref, g):
        turned = d_ref[...].reshape(depth * plane, half).T
        per = nt // 8
        for share in range(nt):
            for tap in range((share % per) * tp, (share % per + 1) * tp):
                if tap >= 27:
                    grad[g, share // 2, share % 2, tap % tp] = jnp.zeros((16, half), BF)
        for i in range(3):
            cols = jnp.concatenate(
                [
                    x[pl.ds(i, depth), pl.ds(j, hy)].reshape(depth * plane, 3 * half)
                    for j in range(3)
                ],
                axis=1,
            )
            out = jnp.dot(turned, cols, preferred_element_type=F32)
            for q in range(9):
                tap = 9 * i + q
                tile = out[:, q * half : (q + 1) * half].T.astype(BF)
                for r in range(8):
                    share = r * per + tap // tp
                    grad[g, share // 2, share % 2, tap % tp] = tile[16 * r : 16 * (r + 1)]

    def level_1(g):
        c = copy(grad.at[g, :, 1 - core], got1.at[g], s, partner)
        c.start()
        return c

    def level_2(g, c):
        c.wait()
        part[g] = (grad[g, :, core].astype(F32) + got1[g].astype(F32)).astype(BF)
        out = []
        for d in range(1, m):
            to = lax.rem(chip + d, m)
            k = copy(part.at[g, to], got2.at[g, d - 1], s, 2 * to + core)
            k.start()
            out.append(k)
        return out

    def level_3(g, cs):
        for c in cs:
            c.wait()
        acc = part[g, chip].astype(F32)
        for d in range(1, m):
            acc = acc + got2[g, d - 1].astype(F32)
        total[g, chip, core] = acc.astype(BF)
        out = []
        for d in range(1, m):
            to = lax.rem(chip + d, m)
            k = copy(total.at[g, chip, core], total.at[g, chip, core], s, 2 * to + core)
            k.start()
            out.append(k)
        return out

    def level_4(g, cs):
        for c in cs:
            c.wait()
        k = copy(total.at[g, :, core], total.at[g, :, core], s, partner)
        k.start()
        return k

    wgrad(xz, pg_s, 1)
    g1 = level_1(1)
    halo_finish(r_halo, 1, xr)

    def recompute_f(z):
        f = jnp.tanh(conv(xr, flat(w, 0, 0), z))
        fz_s[pl.ds(z, step)] = (1.0 - f * f).reshape(step, plane, half)

    each(recompute_f)
    g2 = level_2(1, g1)
    halo_finish(pg_halo, 2, xpg)
    parts["c1"].wait()

    def grad_one(z):
        d1 = (block(c_in, z, 0, 0) + conv(xpg, flat(wt, 1), z)).astype(BF)
        put(igrad, z, 0, d1)
        v = d1.astype(F32) * fz_s[pl.ds(z, step)].reshape(rows, half)
        pf_s[pl.ds(z, step)] = v.astype(BF).reshape(step, plane, half)
        fill(xpf, z + 1, step, v)

    each(grad_one)
    pf_halo = halo_copies(3, mid(xpf, 1), mid(xpf, depth))
    halo_start(pf_halo)
    parts["a2"].wait()
    a_halo = halo_copies(
        4, a_in.at[0, 0, :, :, pl.ds(half, half)], a_in.at[0, depth - 1, :, :, pl.ds(half, half)]
    )
    halo_start(a_halo)
    wgrad(xr, pf_s, 0)
    f1 = level_1(0)
    each(lambda z: fill(xa, z + 1, step, block(a_in, z, 1, 0)))
    halo_finish(a_halo, 4, xa)
    parts["a1"].wait()
    f2 = level_2(0, f1)

    def forward_one(z):
        b1 = block(a_in, z, 0, 0) + jnp.tanh(conv(xa, flat(w, 0, 0), z))
        put(fwd, z, 0, b1)
        fill(xb, z + 1, step, b1)

    each(forward_one)
    b_halo = halo_copies(5, mid(xb, 1), mid(xb, depth))
    halo_start(b_halo)
    g3 = level_3(1, g2)
    halo_finish(pf_halo, 3, xpf)
    each(lambda z: put(igrad, z, 1, block(c_in, z, 1, 0) + conv(xpf, flat(wt, 0), z)))
    f3 = level_3(0, f2)
    halo_finish(b_halo, 5, xb)
    each(
        lambda z: put(
            fwd, z, 1, block(a_in, z, 1, 0) + jnp.tanh(conv(xb, flat(w, 0, 1), z))
        )
    )
    g4 = level_4(1, g3)
    f4 = level_4(0, f3)
    g4.wait()
    gsum[1] = total[1]
    f4.wait()
    gsum[0] = total[0]


def shards(carried_act, stored_out, cotangent, weights, momentum):
    ns, nt = lax.axis_size("section"), lax.axis_size("tile")
    _, depth, hy, wx, chans = stored_out.shape
    half = chans // 2
    per = nt // 8
    tp = -(-27 // per)
    m = nt // 2
    step = 2 if depth % 2 == 0 else 1
    field = (depth + 2, hy + 2, wx, 3 * half)
    sems = 12 + 4 + 2 * (2 + 2 * (m - 1))
    vm = pltpu.VMEM
    cells = depth * hy * wx
    flops = 16 * cells * 27 * half * half
    fwd, igrad, gsum = pl.pallas_call(
        functools.partial(kernel, ns, nt, tp, step),
        out_shape=(
            jax.ShapeDtypeStruct((depth, hy, wx, chans), BF),
            jax.ShapeDtypeStruct((depth, hy, wx, chans), BF),
            jax.ShapeDtypeStruct((2, m, 2, tp, 16, half), BF),
        ),
        in_specs=[
            pl.BlockSpec(memory_space=pl.ANY),
            pl.BlockSpec(memory_space=vm),
            pl.BlockSpec(memory_space=pl.ANY),
            pl.BlockSpec(memory_space=vm),
        ],
        out_specs=[pl.BlockSpec(memory_space=vm)] * 3,
        scratch_shapes=[vm(field, BF)] * 6
        + [
            vm((6, 2, hy, wx, half), BF),
            vm((1, depth, hy, wx, chans), BF),
            vm((1, depth, hy, wx, chans), BF),
            vm((depth, hy * wx, half), F32),
            vm((depth, hy * wx, half), F32),
            vm((2, 27, half, half), BF),
            vm((depth, hy * wx, half), BF),
            vm((depth, hy * wx, half), BF),
            vm((2, m, 2, tp, 16, half), BF),
            vm((2, m, tp, 16, half), BF),
            vm((2, m, tp, 16, half), BF),
            vm((2, m - 1, tp, 16, half), BF),
            vm((2, m, 2, tp, 16, half), BF),
            pltpu.SemaphoreType.DMA((sems,)),
            pltpu.SemaphoreType.DMA((sems,)),
        ],
        compiler_params=pltpu.CompilerParams(
            collective_id=0, has_side_effects=True, vmem_limit_bytes=56 * 1024 * 1024
        ),
        cost_estimate=pl.CostEstimate(
            flops=flops, bytes_accessed=12 * 1024 * 1024, transcendentals=4 * cells * half
        ),
    )(carried_act, stored_out, cotangent, weights)
    count = depth * nt * hy * wx
    scale = grad_weight / jnp.sqrt(jnp.float32(count))
    grads = gsum.reshape(2, 8, per * tp, 16, half)[:, :, :27]
    grads = jnp.transpose(grads, (0, 2, 1, 3, 4)).reshape(momentum.shape)
    new_momentum = momentum_decay * momentum + grads.astype(F32) * scale
    return (fwd[None], igrad[None], new_momentum)


def solution(mesh):
    field = P("section", "tile", None, None, None)
    held = P("section", None, None, None, None)
    return jax.shard_map(
        shards,
        mesh=mesh,
        in_specs=(field, field, field, held, held),
        out_specs=(field, field, held),
        check_vma=False,
    )
```

```python
import functools

import jax
import jax.numpy as jnp
from jax import lax
from jax.experimental import pallas as pl
from jax.experimental.pallas import tpu as pltpu
from jax.sharding import PartitionSpec as P

momentum_decay = 0.9
grad_weight = 0.25
BF = jnp.bfloat16
F32 = jnp.float32


def kernel(
    ns, nt, tp, step,
    act, stored, cot, w,
    fwd, igrad, gsum,
    xz, xr, xpg, xpf, xa, xb, halo, a_in, c_in, gz_s, fz_s, wt, pg_s, pf_s,
    grad, got1, part, got2, total, send, recv,
):
    depth, hy, wx = a_in.shape[1:4]
    half = w.shape[-1]
    s = lax.axis_index("section")
    t = lax.axis_index("tile")
    m = nt // 2
    chip, core = t // 2, lax.rem(t, 2)
    partner = 2 * chip + (1 - core)
    nxt, prv = lax.rem(s + 1, ns), lax.rem(s + ns - 1, ns)
    has_low, has_high = t > 0, t < nt - 1
    plane = hy * wx
    rows = step * plane
    steps = depth // step
    used = [0]

    def at(sec, tile):
        return {"section": sec, "tile": tile}

    def copy(src, dst, sec, tile):
        i = used[0]
        used[0] += 1
        return pltpu.make_async_remote_copy(
            src_ref=src, dst_ref=dst, send_sem=send.at[i], recv_sem=recv.at[i],
            device_id=at(sec, tile), device_id_type=pl.DeviceIdType.MESH,
        )

    barrier = pltpu.get_barrier_semaphore()

    def hail(sec, tile):
        pl.semaphore_signal(
            barrier, inc=1, device_id=at(sec, tile), device_id_type=pl.DeviceIdType.MESH
        )

    hail(nxt, t)
    hail(prv, t)
    for d in range(1, m):
        hail(s, lax.rem(t + 2 * d, nt))

    hail(s, lax.rem(t + 1, nt))
    hail(s, lax.rem(t + nt - 1, nt))
    pl.semaphore_wait(barrier, m + 3)

    def mid(x, z):
        return x.at[z, pl.ds(1, hy), :, pl.ds(half, half)]

    def halo_copies(slot, first, last):
        down = copy(first, halo.at[slot, 1], s, lax.rem(t + nt - 1, nt))
        up = copy(last, halo.at[slot, 0], s, lax.rem(t + 1, nt))
        return down, up

    def halo_start(pair):
        @pl.when(has_low)
        def _():
            pair[0].start()

        @pl.when(has_high)
        def _():
            pair[1].start()

    def fill(x, z, count, value):
        n = count * plane
        value = value.reshape(n, half)
        col = lax.rem(lax.broadcasted_iota(jnp.int32, (n, half), 0), wx)
        left = jnp.where(col == 0, 0.0, pltpu.roll(value, 1, 0))
        right = jnp.where(col == wx - 1, 0.0, pltpu.roll(value, n - 1, 0))
        for k, v in enumerate((left, value, right)):
            x[pl.ds(z, count), pl.ds(1, hy), :, pl.ds(k * half, half)] = (
                v.astype(BF).reshape(count, hy, wx, half)
            )

    def halo_finish(pair, slot, x):
        @pl.when(has_low)
        def _():
            pair[0].wait_send()
            pair[1].wait_recv()
            fill(x, 0, 1, halo[slot, 0].astype(F32))

        @pl.when(has_high)
        def _():
            pair[1].wait_send()
            pair[0].wait_recv()
            fill(x, depth + 1, 1, halo[slot, 1].astype(F32))

    def clear(x):
        edge = jnp.zeros((depth + 2, 1, wx, 3 * half), BF)
        x[:, pl.ds(0, 1)] = edge
        x[:, pl.ds(hy + 1, 1)] = edge
        empty = jnp.zeros((1, hy, wx, 3 * half), BF)

        @pl.when(t == 0)
        def _():
            x[pl.ds(0, 1), pl.ds(1, hy)] = empty

        @pl.when(t == nt - 1)
        def _():
            x[pl.ds(depth + 1, 1), pl.ds(1, hy)] = empty

    def conv(x, weight, z):
        cols = jnp.concatenate(
            [
                x[pl.ds(z + i, step), pl.ds(j, hy)].reshape(rows, 3 * half)
                for i in range(3)
                for j in range(3)
            ],
            axis=1,
        )
        return jnp.dot(cols, weight, preferred_element_type=F32)

    def block(ref, z, part_at, *lead):
        return ref[(*lead, pl.ds(z, step), slice(None), slice(None), pl.ds(part_at * half, half))].astype(
            F32
        ).reshape(rows, half)

    def put(ref, z, part_at, value):
        ref[pl.ds(z, step), :, :, pl.ds(part_at * half, half)] = value.astype(BF).reshape(
            step, hy, wx, half
        )

    def each(body):
        def run(n, carry):
            body(n * step)
            return carry

        lax.fori_loop(0, steps, run, 0)

    z_halo = halo_copies(
        0, stored.at[0, 0, :, :, pl.ds(0, half)], stored.at[0, depth - 1, :, :, pl.ds(0, half)]
    )
    halo_start(z_halo)
    parts = {}
    for name, src, dst, target, piece in (
        ("c2", cot, c_in, prv, 1),
        ("c1", cot, c_in, prv, 0),
        ("a2", act, a_in, nxt, 1),
        ("a1", act, a_in, nxt, 0),
    ):
        view = (0, slice(None), slice(None), slice(None), pl.ds(piece * half, half))
        parts[name] = copy(src.at[view], dst.at[view], target, t)

    parts["c2"].start()
    for x in (xz, xr, xpg, xpf, xa, xb):
        clear(x)
    each(lambda z: fill(xz, z + 1, step, block(stored, z, 0, 0)))

    def turn(n, carry):
        for which in range(2):
            wt[which, n] = w[0, which, 26 - n].T
        return carry

    lax.fori_loop(0, 27, turn, 0)
    halo_finish(z_halo, 0, xz)

    def flat(ref, *lead):
        return ref[lead].reshape(27 * half, half)

    def reconstruct(z):
        g = jnp.tanh(conv(xz, flat(w, 0, 1), z))
        gz_s[pl.ds(z, step)] = (1.0 - g * g).reshape(step, plane, half)
        fill(xr, z + 1, step, block(stored, z, 1, 0) - g)

    each(reconstruct)
    r_halo = halo_copies(1, mid(xr, 1), mid(xr, depth))
    halo_start(r_halo)
    parts["c2"].wait_send()
    parts["c1"].start()
    parts["c2"].wait_recv()

    def pre_g(z):
        v = block(c_in, z, 1, 0) * gz_s[pl.ds(z, step)].reshape(rows, half)
        pg_s[pl.ds(z, step)] = v.astype(BF).reshape(step, plane, half)
        fill(xpg, z + 1, step, v)

    each(pre_g)
    pg_halo = halo_copies(2, mid(xpg, 1), mid(xpg, depth))
    halo_start(pg_halo)

    def wgrad(x, d_ref, g):
        turned = d_ref[...].reshape(depth * plane, half).T
        per = nt // 8
        for share in range(nt):
            for tap in range((share % per) * tp, (share % per + 1) * tp):
                if tap >= 27:
                    grad[g, share // 2, share % 2, tap % tp] = jnp.zeros((16, half), BF)
        for i in range(3):
            cols = jnp.concatenate(
                [
                    x[pl.ds(i, depth), pl.ds(j, hy)].reshape(depth * plane, 3 * half)
                    for j in range(3)
                ],
                axis=1,
            )
            out = jnp.dot(turned, cols, preferred_element_type=F32)
            for q in range(9):
                tap = 9 * i + q
                tile = out[:, q * half : (q + 1) * half].T.astype(BF)
                for r in range(8):
                    share = r * per + tap // tp
                    grad[g, share // 2, share % 2, tap % tp] = tile[16 * r : 16 * (r + 1)]

    def level_1(g):
        c = copy(grad.at[g, :, 1 - core], got1.at[g], s, partner)
        c.start()
        return c

    def level_2(g, c):
        c.wait()
        part[g] = (grad[g, :, core].astype(F32) + got1[g].astype(F32)).astype(BF)
        out = []
        for d in range(1, m):
            to = lax.rem(chip + d, m)
            k = copy(part.at[g, to], got2.at[g, d - 1], s, 2 * to + core)
            k.start()
            out.append(k)
        return out

    def level_3(g, cs):
        for c in cs:
            c.wait()
        acc = part[g, chip].astype(F32)
        for d in range(1, m):
            acc = acc + got2[g, d - 1].astype(F32)
        total[g, chip, core] = acc.astype(BF)
        out = []
        for d in range(1, m):
            to = lax.rem(chip + d, m)
            k = copy(total.at[g, chip, core], total.at[g, chip, core], s, 2 * to + core)
            k.start()
            out.append(k)
        return out

    def level_4(g, cs):
        for c in cs:
            c.wait()
        k = copy(total.at[g, :, core], total.at[g, :, core], s, partner)
        k.start()
        return k

    wgrad(xz, pg_s, 1)
    g1 = level_1(1)
    halo_finish(r_halo, 1, xr)

    def recompute_f(z):
        f = jnp.tanh(conv(xr, flat(w, 0, 0), z))
        fz_s[pl.ds(z, step)] = (1.0 - f * f).reshape(step, plane, half)

    each(recompute_f)
    g2 = level_2(1, g1)
    halo_finish(pg_halo, 2, xpg)
    parts["c1"].wait_send()
    parts["a2"].start()
    parts["c1"].wait_recv()

    def grad_one(z):
        d1 = (block(c_in, z, 0, 0) + conv(xpg, flat(wt, 1), z)).astype(BF)
        put(igrad, z, 0, d1)
        v = d1.astype(F32) * fz_s[pl.ds(z, step)].reshape(rows, half)
        pf_s[pl.ds(z, step)] = v.astype(BF).reshape(step, plane, half)
        fill(xpf, z + 1, step, v)

    each(grad_one)
    pf_halo = halo_copies(3, mid(xpf, 1), mid(xpf, depth))
    halo_start(pf_halo)
    wgrad(xr, pf_s, 0)
    f1 = level_1(0)
    parts["a2"].wait_send()
    parts["a1"].start()
    g3 = level_3(1, g2)
    halo_finish(pf_halo, 3, xpf)
    each(lambda z: put(igrad, z, 1, block(c_in, z, 1, 0) + conv(xpf, flat(wt, 0), z)))
    f2 = level_2(0, f1)
    parts["a2"].wait_recv()
    a_halo = halo_copies(
        4, a_in.at[0, 0, :, :, pl.ds(half, half)], a_in.at[0, depth - 1, :, :, pl.ds(half, half)]
    )
    halo_start(a_halo)
    each(lambda z: fill(xa, z + 1, step, block(a_in, z, 1, 0)))
    halo_finish(a_halo, 4, xa)

    def forward_conv(z):
        gz_s[pl.ds(z, step)] = jnp.tanh(conv(xa, flat(w, 0, 0), z)).reshape(step, plane, half)

    each(forward_conv)
    parts["a1"].wait()

    def forward_one(z):
        b1 = block(a_in, z, 0, 0) + gz_s[pl.ds(z, step)].reshape(rows, half)
        put(fwd, z, 0, b1)
        fill(xb, z + 1, step, b1)

    each(forward_one)
    b_halo = halo_copies(5, mid(xb, 1), mid(xb, depth))
    halo_start(b_halo)
    f3 = level_3(0, f2)
    g4 = level_4(1, g3)
    halo_finish(b_halo, 5, xb)
    each(
        lambda z: put(
            fwd, z, 1, block(a_in, z, 1, 0) + jnp.tanh(conv(xb, flat(w, 0, 1), z))
        )
    )

    def lay_out(g):
        per = nt // 8
        for share in range(nt):
            r, first = share // per, (share % per) * tp
            count = min(27 - first, tp)
            gsum[g, pl.ds(first, count), pl.ds(16 * r, 16)] = total[
                g, share // 2, share % 2, pl.ds(0, count)
            ]

    g4.wait()
    lay_out(1)
    level_4(0, f3).wait()
    lay_out(0)


def shards(carried_act, stored_out, cotangent, weights, momentum):
    ns, nt = lax.axis_size("section"), lax.axis_size("tile")
    _, depth, hy, wx, chans = stored_out.shape
    half = chans // 2
    per = nt // 8
    tp = -(-27 // per)
    m = nt // 2
    step = 2 if depth % 2 == 0 else 1
    field = (depth + 2, hy + 2, wx, 3 * half)
    sems = 12 + 4 + 2 * (2 + 2 * (m - 1))
    vm = pltpu.VMEM
    cells = depth * hy * wx
    flops = 16 * cells * 27 * half * half
    fwd, igrad, gsum = pl.pallas_call(
        functools.partial(kernel, ns, nt, tp, step),
        out_shape=(
            jax.ShapeDtypeStruct((depth, hy, wx, chans), BF),
            jax.ShapeDtypeStruct((depth, hy, wx, chans), BF),
            jax.ShapeDtypeStruct((2, 27, half, half), BF),
        ),
        in_specs=[
            pl.BlockSpec(memory_space=pl.ANY),
            pl.BlockSpec(memory_space=vm),
            pl.BlockSpec(memory_space=pl.ANY),
            pl.BlockSpec(memory_space=vm),
        ],
        out_specs=[pl.BlockSpec(memory_space=vm)] * 3,
        scratch_shapes=[vm(field, BF)] * 6
        + [
            vm((6, 2, hy, wx, half), BF),
            vm((1, depth, hy, wx, chans), BF),
            vm((1, depth, hy, wx, chans), BF),
            vm((depth, hy * wx, half), F32),
            vm((depth, hy * wx, half), F32),
            vm((2, 27, half, half), BF),
            vm((depth, hy * wx, half), BF),
            vm((depth, hy * wx, half), BF),
            vm((2, m, 2, tp, 16, half), BF),
            vm((2, m, tp, 16, half), BF),
            vm((2, m, tp, 16, half), BF),
            vm((2, m - 1, tp, 16, half), BF),
            vm((2, m, 2, tp, 16, half), BF),
            pltpu.SemaphoreType.DMA((sems,)),
            pltpu.SemaphoreType.DMA((sems,)),
        ],
        compiler_params=pltpu.CompilerParams(
            collective_id=0, has_side_effects=True, vmem_limit_bytes=56 * 1024 * 1024
        ),
        cost_estimate=pl.CostEstimate(
            flops=flops, bytes_accessed=12 * 1024 * 1024, transcendentals=4 * cells * half
        ),
    )(carried_act, stored_out, cotangent, weights)
    count = depth * nt * hy * wx
    scale = grad_weight / jnp.sqrt(jnp.float32(count))
    new_momentum = momentum_decay * momentum + gsum[None].astype(F32) * scale
    return (fwd[None], igrad[None], new_momentum)


def solution(mesh):
    field = P("section", "tile", None, None, None)
    held = P("section", None, None, None, None)
    return jax.shard_map(
        shards,
        mesh=mesh,
        in_specs=(field, field, field, held, held),
        out_specs=(field, field, held),
        check_vma=False,
    )
```

```python
import functools

import jax
import jax.numpy as jnp
from jax import lax
from jax.experimental import pallas as pl
from jax.experimental.pallas import tpu as pltpu
from jax.sharding import PartitionSpec as P

momentum_decay = 0.9
grad_weight = 0.25
BF = jnp.bfloat16
F32 = jnp.float32


def kernel(
    ns, nt, tp, step,
    act, stored, cot, w,
    fwd, igrad, gsum,
    xz, xr, xpg, xpf, xa, xb, halo, a_in, c_in, gz_s, fz_s, wt, pg_s, pf_s,
    grad, got1, part, got2, total, send, recv,
):
    depth, hy, wx = a_in.shape[1:4]
    half = w.shape[-1]
    s = lax.axis_index("section")
    t = lax.axis_index("tile")
    m = nt // 2
    chip, core = t // 2, lax.rem(t, 2)
    partner = 2 * chip + (1 - core)
    nxt, prv = lax.rem(s + 1, ns), lax.rem(s + ns - 1, ns)
    has_low, has_high = t > 0, t < nt - 1
    plane = hy * wx
    rows = step * plane
    steps = depth // step
    used = [0]

    def at(sec, tile):
        return {"section": sec, "tile": tile}

    def copy(src, dst, sec, tile):
        i = used[0]
        used[0] += 1
        return pltpu.make_async_remote_copy(
            src_ref=src, dst_ref=dst, send_sem=send.at[i], recv_sem=recv.at[i],
            device_id=at(sec, tile), device_id_type=pl.DeviceIdType.MESH,
        )

    barrier = pltpu.get_barrier_semaphore()

    def hail(sec, tile):
        pl.semaphore_signal(
            barrier, inc=1, device_id=at(sec, tile), device_id_type=pl.DeviceIdType.MESH
        )

    hail(nxt, t)
    hail(prv, t)
    for d in range(1, m):
        hail(s, lax.rem(t + 2 * d, nt))

    hail(s, lax.rem(t + 1, nt))
    hail(s, lax.rem(t + nt - 1, nt))
    pl.semaphore_wait(barrier, m + 3)

    def mid(x, z):
        return x.at[z, pl.ds(1, hy), :, pl.ds(half, half)]

    def halo_copies(slot, first, last):
        down = copy(first, halo.at[slot, 1], s, lax.rem(t + nt - 1, nt))
        up = copy(last, halo.at[slot, 0], s, lax.rem(t + 1, nt))
        return down, up

    def halo_start(pair):
        @pl.when(has_low)
        def _():
            pair[0].start()

        @pl.when(has_high)
        def _():
            pair[1].start()

    def fill(x, z, count, value):
        n = count * plane
        value = value.reshape(n, half)
        col = lax.rem(lax.broadcasted_iota(jnp.int32, (n, half), 0), wx)
        left = jnp.where(col == 0, 0.0, pltpu.roll(value, 1, 0))
        right = jnp.where(col == wx - 1, 0.0, pltpu.roll(value, n - 1, 0))
        for k, v in enumerate((left, value, right)):
            x[pl.ds(z, count), pl.ds(1, hy), :, pl.ds(k * half, half)] = (
                v.astype(BF).reshape(count, hy, wx, half)
            )

    def halo_finish(pair, slot, x):
        @pl.when(has_low)
        def _():
            pair[0].wait_send()
            pair[1].wait_recv()
            fill(x, 0, 1, halo[slot, 0].astype(F32))

        @pl.when(has_high)
        def _():
            pair[1].wait_send()
            pair[0].wait_recv()
            fill(x, depth + 1, 1, halo[slot, 1].astype(F32))

    def clear(x):
        edge = jnp.zeros((depth + 2, 1, wx, 3 * half), BF)
        x[:, pl.ds(0, 1)] = edge
        x[:, pl.ds(hy + 1, 1)] = edge
        empty = jnp.zeros((1, hy, wx, 3 * half), BF)

        @pl.when(t == 0)
        def _():
            x[pl.ds(0, 1), pl.ds(1, hy)] = empty

        @pl.when(t == nt - 1)
        def _():
            x[pl.ds(depth + 1, 1), pl.ds(1, hy)] = empty

    def conv(x, weight, z):
        cols = jnp.concatenate(
            [
                x[pl.ds(z + i, step), pl.ds(j, hy)].reshape(rows, 3 * half)
                for i in range(3)
                for j in range(3)
            ],
            axis=1,
        )
        return jnp.dot(cols, weight, preferred_element_type=F32)

    def block(ref, z, part_at, *lead):
        return ref[(*lead, pl.ds(z, step), slice(None), slice(None), pl.ds(part_at * half, half))].astype(
            F32
        ).reshape(rows, half)

    def put(ref, z, part_at, value):
        ref[pl.ds(z, step), :, :, pl.ds(part_at * half, half)] = value.astype(BF).reshape(
            step, hy, wx, half
        )

    def each(body):
        def run(n, carry):
            body(n * step)
            return carry

        lax.fori_loop(0, steps, run, 0)

    z_halo = halo_copies(
        0, stored.at[0, 0, :, :, pl.ds(0, half)], stored.at[0, depth - 1, :, :, pl.ds(0, half)]
    )
    halo_start(z_halo)
    parts = {}
    for name, src, dst, target, piece in (
        ("c2", cot, c_in, prv, 1),
        ("c1", cot, c_in, prv, 0),
        ("a2", act, a_in, nxt, 1),
        ("a1", act, a_in, nxt, 0),
    ):
        view = (0, slice(None), slice(None), slice(None), pl.ds(piece * half, half))
        parts[name] = copy(src.at[view], dst.at[view], target, t)

    parts["c2"].start()
    for x in (xz, xr, xpg, xpf, xa, xb):
        clear(x)
    each(lambda z: fill(xz, z + 1, step, block(stored, z, 0, 0)))

    def turn(n, carry):
        for which in range(2):
            wt[which, n] = w[0, which, 26 - n].T
        return carry

    halo_finish(z_halo, 0, xz)

    def flat(ref, *lead):
        return ref[lead].reshape(27 * half, half)

    def reconstruct(z):
        g = jnp.tanh(conv(xz, flat(w, 0, 1), z))
        gz_s[pl.ds(z, step)] = (1.0 - g * g).reshape(step, plane, half)
        fill(xr, z + 1, step, block(stored, z, 1, 0) - g)

    each(reconstruct)
    r_halo = halo_copies(1, mid(xr, 1), mid(xr, depth))
    halo_start(r_halo)
    parts["c2"].wait_send()
    parts["c1"].start()
    lax.fori_loop(0, 27, turn, 0)
    parts["c2"].wait_recv()

    def pre_g(z):
        v = block(c_in, z, 1, 0) * gz_s[pl.ds(z, step)].reshape(rows, half)
        pg_s[pl.ds(z, step)] = v.astype(BF).reshape(step, plane, half)
        fill(xpg, z + 1, step, v)

    each(pre_g)
    pg_halo = halo_copies(2, mid(xpg, 1), mid(xpg, depth))
    halo_start(pg_halo)

    def wgrad(x, d_ref, g):
        turned = d_ref[...].reshape(depth * plane, half).T
        per = nt // 8
        for share in range(nt):
            for tap in range((share % per) * tp, (share % per + 1) * tp):
                if tap >= 27:
                    grad[g, share // 2, share % 2, tap % tp] = jnp.zeros((16, half), BF)
        for i in range(3):
            cols = jnp.concatenate(
                [
                    x[pl.ds(i, depth), pl.ds(j, hy)].reshape(depth * plane, 3 * half)
                    for j in range(3)
                ],
                axis=1,
            )
            out = jnp.dot(turned, cols, preferred_element_type=F32)
            for q in range(9):
                tap = 9 * i + q
                tile = out[:, q * half : (q + 1) * half].T.astype(BF)
                for r in range(8):
                    share = r * per + tap // tp
                    grad[g, share // 2, share % 2, tap % tp] = tile[16 * r : 16 * (r + 1)]

    def level_1(g):
        c = copy(grad.at[g, :, 1 - core], got1.at[g], s, partner)
        c.start()
        return c

    def level_2(g, c):
        c.wait()
        part[g] = (grad[g, :, core].astype(F32) + got1[g].astype(F32)).astype(BF)
        out = []
        for d in range(1, m):
            to = lax.rem(chip + d, m)
            k = copy(part.at[g, to], got2.at[g, d - 1], s, 2 * to + core)
            k.start()
            out.append(k)
        return out

    def level_3(g, cs):
        for c in cs:
            c.wait()
        acc = part[g, chip].astype(F32)
        for d in range(1, m):
            acc = acc + got2[g, d - 1].astype(F32)
        total[g, chip, core] = acc.astype(BF)
        out = []
        for d in range(1, m):
            to = lax.rem(chip + d, m)
            k = copy(total.at[g, chip, core], total.at[g, chip, core], s, 2 * to + core)
            k.start()
            out.append(k)
        return out

    def level_4(g, cs):
        for c in cs:
            c.wait()
        k = copy(total.at[g, :, core], total.at[g, :, core], s, partner)
        k.start()
        return k

    wgrad(xz, pg_s, 1)
    g1 = level_1(1)
    halo_finish(r_halo, 1, xr)

    def recompute_f(z):
        f = jnp.tanh(conv(xr, flat(w, 0, 0), z))
        fz_s[pl.ds(z, step)] = (1.0 - f * f).reshape(step, plane, half)

    each(recompute_f)
    g2 = level_2(1, g1)
    halo_finish(pg_halo, 2, xpg)
    parts["c1"].wait_send()
    parts["a2"].start()
    parts["c1"].wait_recv()

    def grad_one(z):
        d1 = (block(c_in, z, 0, 0) + conv(xpg, flat(wt, 1), z)).astype(BF)
        put(igrad, z, 0, d1)
        v = d1.astype(F32) * fz_s[pl.ds(z, step)].reshape(rows, half)
        pf_s[pl.ds(z, step)] = v.astype(BF).reshape(step, plane, half)
        fill(xpf, z + 1, step, v)

    each(grad_one)
    pf_halo = halo_copies(3, mid(xpf, 1), mid(xpf, depth))
    halo_start(pf_halo)
    wgrad(xr, pf_s, 0)
    f1 = level_1(0)
    parts["a2"].wait_send()
    parts["a1"].start()
    g3 = level_3(1, g2)
    halo_finish(pf_halo, 3, xpf)
    f2 = level_2(0, f1)
    each(lambda z: put(igrad, z, 1, block(c_in, z, 1, 0) + conv(xpf, flat(wt, 0), z)))
    g4 = level_4(1, g3)
    parts["a2"].wait_recv()
    a_halo = halo_copies(
        4, a_in.at[0, 0, :, :, pl.ds(half, half)], a_in.at[0, depth - 1, :, :, pl.ds(half, half)]
    )
    halo_start(a_halo)
    each(lambda z: fill(xa, z + 1, step, block(a_in, z, 1, 0)))
    halo_finish(a_halo, 4, xa)

    def forward_conv(z):
        gz_s[pl.ds(z, step)] = jnp.tanh(conv(xa, flat(w, 0, 0), z)).reshape(step, plane, half)

    each(forward_conv)
    f3 = level_3(0, f2)
    parts["a1"].wait()

    def forward_one(z):
        b1 = block(a_in, z, 0, 0) + gz_s[pl.ds(z, step)].reshape(rows, half)
        put(fwd, z, 0, b1)
        fill(xb, z + 1, step, b1)

    each(forward_one)
    b_halo = halo_copies(5, mid(xb, 1), mid(xb, depth))
    halo_start(b_halo)
    halo_finish(b_halo, 5, xb)
    each(
        lambda z: put(
            fwd, z, 1, block(a_in, z, 1, 0) + jnp.tanh(conv(xb, flat(w, 0, 1), z))
        )
    )

    def lay_out(g):
        per = nt // 8
        for share in range(nt):
            r, first = share // per, (share % per) * tp
            count = min(27 - first, tp)
            gsum[g, pl.ds(first, count), pl.ds(16 * r, 16)] = total[
                g, share // 2, share % 2, pl.ds(0, count)
            ]

    g4.wait()
    lay_out(1)
    level_4(0, f3).wait()
    lay_out(0)


def shards(carried_act, stored_out, cotangent, weights, momentum):
    ns, nt = lax.axis_size("section"), lax.axis_size("tile")
    _, depth, hy, wx, chans = stored_out.shape
    half = chans // 2
    per = nt // 8
    tp = -(-27 // per)
    m = nt // 2
    step = 3 if depth % 3 == 0 else 1
    field = (depth + 2, hy + 2, wx, 3 * half)
    sems = 12 + 4 + 2 * (2 + 2 * (m - 1))
    vm = pltpu.VMEM
    cells = depth * hy * wx
    flops = 16 * cells * 27 * half * half
    fwd, igrad, gsum = pl.pallas_call(
        functools.partial(kernel, ns, nt, tp, step),
        out_shape=(
            jax.ShapeDtypeStruct((depth, hy, wx, chans), BF),
            jax.ShapeDtypeStruct((depth, hy, wx, chans), BF),
            jax.ShapeDtypeStruct((2, 27, half, half), BF),
        ),
        in_specs=[
            pl.BlockSpec(memory_space=pl.ANY),
            pl.BlockSpec(memory_space=vm),
            pl.BlockSpec(memory_space=pl.ANY),
            pl.BlockSpec(memory_space=vm),
        ],
        out_specs=[pl.BlockSpec(memory_space=vm)] * 3,
        scratch_shapes=[vm(field, BF)] * 6
        + [
            vm((6, 2, hy, wx, half), BF),
            vm((1, depth, hy, wx, chans), BF),
            vm((1, depth, hy, wx, chans), BF),
            vm((depth, hy * wx, half), F32),
            vm((depth, hy * wx, half), F32),
            vm((2, 27, half, half), BF),
            vm((depth, hy * wx, half), BF),
            vm((depth, hy * wx, half), BF),
            vm((2, m, 2, tp, 16, half), BF),
            vm((2, m, tp, 16, half), BF),
            vm((2, m, tp, 16, half), BF),
            vm((2, m - 1, tp, 16, half), BF),
            vm((2, m, 2, tp, 16, half), BF),
            pltpu.SemaphoreType.DMA((sems,)),
            pltpu.SemaphoreType.DMA((sems,)),
        ],
        compiler_params=pltpu.CompilerParams(
            collective_id=0, has_side_effects=True, vmem_limit_bytes=56 * 1024 * 1024
        ),
        cost_estimate=pl.CostEstimate(
            flops=flops, bytes_accessed=12 * 1024 * 1024, transcendentals=4 * cells * half
        ),
    )(carried_act, stored_out, cotangent, weights)
    count = depth * nt * hy * wx
    scale = grad_weight / jnp.sqrt(jnp.float32(count))
    new_momentum = momentum_decay * momentum + gsum[None].astype(F32) * scale
    return (fwd[None], igrad[None], new_momentum)


def solution(mesh):
    field = P("section", "tile", None, None, None)
    held = P("section", None, None, None, None)
    return jax.shard_map(
        shards,
        mesh=mesh,
        in_specs=(field, field, field, held, held),
        out_specs=(field, field, held),
        check_vma=False,
    )
```

```python
import functools

import jax
import jax.numpy as jnp
from jax import lax
from jax.experimental import pallas as pl
from jax.experimental.pallas import tpu as pltpu
from jax.sharding import PartitionSpec as P

momentum_decay = 0.9
grad_weight = 0.25
BF = jnp.bfloat16
F32 = jnp.float32


def kernel(
    ns, nt, tp, step,
    act, stored, cot, w,
    fwd, igrad, gsum,
    xz, xr, xpg, xpf, xa, xb, halo, a_in, c_in, gz_s, fz_s, wt, pg_s, pf_s,
    grad, got1, part, got2, total, send, recv,
):
    depth, hy, wx = a_in.shape[1:4]
    half = w.shape[-1]
    s = lax.axis_index("section")
    t = lax.axis_index("tile")
    m = nt // 2
    chip, core = t // 2, lax.rem(t, 2)
    partner = 2 * chip + (1 - core)
    nxt, prv = lax.rem(s + 1, ns), lax.rem(s + ns - 1, ns)
    has_low, has_high = t > 0, t < nt - 1
    plane = hy * wx
    rows = step * plane
    steps = depth // step
    used = [0]

    def at(sec, tile):
        return {"section": sec, "tile": tile}

    def copy(src, dst, sec, tile):
        i = used[0]
        used[0] += 1
        return pltpu.make_async_remote_copy(
            src_ref=src, dst_ref=dst, send_sem=send.at[i], recv_sem=recv.at[i],
            device_id=at(sec, tile), device_id_type=pl.DeviceIdType.MESH,
        )

    barrier = pltpu.get_barrier_semaphore()

    def hail(sec, tile):
        pl.semaphore_signal(
            barrier, inc=1, device_id=at(sec, tile), device_id_type=pl.DeviceIdType.MESH
        )

    hail(nxt, t)
    hail(prv, t)
    for d in range(1, m):
        hail(s, lax.rem(t + 2 * d, nt))

    hail(s, lax.rem(t + 1, nt))
    hail(s, lax.rem(t + nt - 1, nt))
    pl.semaphore_wait(barrier, m + 3)

    def mid(x, z):
        return x.at[z, pl.ds(1, hy), :, pl.ds(half, half)]

    def halo_copies(slot, first, last):
        down = copy(first, halo.at[slot, 1], s, lax.rem(t + nt - 1, nt))
        up = copy(last, halo.at[slot, 0], s, lax.rem(t + 1, nt))
        return down, up

    def halo_start(pair):
        @pl.when(has_low)
        def _():
            pair[0].start()

        @pl.when(has_high)
        def _():
            pair[1].start()

    def fill(x, z, count, value):
        n = count * plane
        value = value.reshape(n, half)
        col = lax.rem(lax.broadcasted_iota(jnp.int32, (n, half), 0), wx)
        left = jnp.where(col == 0, 0.0, pltpu.roll(value, 1, 0))
        right = jnp.where(col == wx - 1, 0.0, pltpu.roll(value, n - 1, 0))
        for k, v in enumerate((left, value, right)):
            x[pl.ds(z, count), pl.ds(1, hy), :, pl.ds(k * half, half)] = (
                v.astype(BF).reshape(count, hy, wx, half)
            )

    def halo_finish(pair, slot, x):
        @pl.when(has_low)
        def _():
            pair[0].wait_send()
            pair[1].wait_recv()
            fill(x, 0, 1, halo[slot, 0].astype(F32))

        @pl.when(has_high)
        def _():
            pair[1].wait_send()
            pair[0].wait_recv()
            fill(x, depth + 1, 1, halo[slot, 1].astype(F32))

    def clear(x):
        edge = jnp.zeros((depth + 2, 1, wx, 3 * half), BF)
        x[:, pl.ds(0, 1)] = edge
        x[:, pl.ds(hy + 1, 1)] = edge
        empty = jnp.zeros((1, hy, wx, 3 * half), BF)

        @pl.when(t == 0)
        def _():
            x[pl.ds(0, 1), pl.ds(1, hy)] = empty

        @pl.when(t == nt - 1)
        def _():
            x[pl.ds(depth + 1, 1), pl.ds(1, hy)] = empty

    def conv(x, weight, z):
        cols = jnp.concatenate(
            [
                x[pl.ds(z + i, step), pl.ds(j, hy)].reshape(rows, 3 * half)
                for i in range(3)
                for j in range(3)
            ],
            axis=1,
        )
        return jnp.dot(cols, weight, preferred_element_type=F32)

    def block(ref, z, part_at, *lead):
        return ref[(*lead, pl.ds(z, step), slice(None), slice(None), pl.ds(part_at * half, half))].astype(
            F32
        ).reshape(rows, half)

    def put(ref, z, part_at, value):
        ref[pl.ds(z, step), :, :, pl.ds(part_at * half, half)] = value.astype(BF).reshape(
            step, hy, wx, half
        )

    def each(body):
        def run(n, carry):
            body(n * step)
            return carry

        lax.fori_loop(0, steps, run, 0)

    z_halo = halo_copies(
        0, stored.at[0, 0, :, :, pl.ds(0, half)], stored.at[0, depth - 1, :, :, pl.ds(0, half)]
    )
    halo_start(z_halo)
    parts = {}
    for name, src, dst, target, piece in (
        ("c2", cot, c_in, prv, 1),
        ("c1", cot, c_in, prv, 0),
        ("a2", act, a_in, nxt, 1),
        ("a1", act, a_in, nxt, 0),
    ):
        view = (0, slice(None), slice(None), slice(None), pl.ds(piece * half, half))
        parts[name] = copy(src.at[view], dst.at[view], target, t)

    parts["c2"].start()
    for x in (xz, xr, xpg, xpf, xa, xb):
        clear(x)
    each(lambda z: fill(xz, z + 1, step, block(stored, z, 0, 0)))

    def turn(n, carry):
        for which in range(2):
            wt[which, n] = w[0, which, 26 - n].T
        return carry

    halo_finish(z_halo, 0, xz)

    def flat(ref, *lead):
        return ref[lead].reshape(27 * half, half)

    def reconstruct(z):
        g = jnp.tanh(conv(xz, flat(w, 0, 1), z))
        gz_s[pl.ds(z, step)] = (1.0 - g * g).reshape(step, plane, half)
        fill(xr, z + 1, step, block(stored, z, 1, 0) - g)

    each(reconstruct)
    r_halo = halo_copies(1, mid(xr, 1), mid(xr, depth))
    halo_start(r_halo)
    parts["c2"].wait_send()
    parts["c1"].start()
    lax.fori_loop(0, 27, turn, 0)
    parts["c2"].wait_recv()

    def pre_g(z):
        v = block(c_in, z, 1, 0) * gz_s[pl.ds(z, step)].reshape(rows, half)
        pg_s[pl.ds(z, step)] = v.astype(BF).reshape(step, plane, half)
        fill(xpg, z + 1, step, v)

    each(pre_g)
    pg_halo = halo_copies(2, mid(xpg, 1), mid(xpg, depth))
    halo_start(pg_halo)

    def wgrad(x, d_ref, g):
        turned = d_ref[...].reshape(depth * plane, half).T
        per = nt // 8
        for share in range(nt):
            for tap in range((share % per) * tp, (share % per + 1) * tp):
                if tap >= 27:
                    grad[g, share // 2, share % 2, tap % tp] = jnp.zeros((16, half), BF)
        for i in range(3):
            cols = jnp.concatenate(
                [
                    x[pl.ds(i, depth), pl.ds(j, hy)].reshape(depth * plane, 3 * half)
                    for j in range(3)
                ],
                axis=1,
            )
            out = jnp.dot(turned, cols, preferred_element_type=F32)
            for q in range(9):
                tap = 9 * i + q
                tile = out[:, q * half : (q + 1) * half].T.astype(BF)
                for r in range(8):
                    share = r * per + tap // tp
                    grad[g, share // 2, share % 2, tap % tp] = tile[16 * r : 16 * (r + 1)]

    def level_1(g):
        c = copy(grad.at[g, :, 1 - core], got1.at[g], s, partner)
        c.start()
        return c

    def level_2(g, c):
        c.wait()
        part[g] = (grad[g, :, core].astype(F32) + got1[g].astype(F32)).astype(BF)
        out = []
        for d in range(1, m):
            to = lax.rem(chip + d, m)
            k = copy(part.at[g, to], got2.at[g, d - 1], s, 2 * to + core)
            k.start()
            out.append(k)
        return out

    def level_3(g, cs):
        for c in cs:
            c.wait()
        acc = part[g, chip].astype(F32)
        for d in range(1, m):
            acc = acc + got2[g, d - 1].astype(F32)
        total[g, chip, core] = acc.astype(BF)
        out = []
        for d in range(1, m):
            to = lax.rem(chip + d, m)
            k = copy(total.at[g, chip, core], total.at[g, chip, core], s, 2 * to + core)
            k.start()
            out.append(k)
        return out

    def level_4(g, cs):
        for c in cs:
            c.wait()
        k = copy(total.at[g, :, core], total.at[g, :, core], s, partner)
        k.start()
        return k

    wgrad(xz, pg_s, 1)
    g1 = level_1(1)
    halo_finish(r_halo, 1, xr)

    def recompute_f(z):
        f = jnp.tanh(conv(xr, flat(w, 0, 0), z))
        fz_s[pl.ds(z, step)] = (1.0 - f * f).reshape(step, plane, half)

    each(recompute_f)
    g2 = level_2(1, g1)
    halo_finish(pg_halo, 2, xpg)
    parts["c1"].wait_send()
    parts["a2"].start()
    parts["c1"].wait_recv()

    def grad_one(z):
        d1 = (block(c_in, z, 0, 0) + conv(xpg, flat(wt, 1), z)).astype(BF)
        put(igrad, z, 0, d1)
        v = d1.astype(F32) * fz_s[pl.ds(z, step)].reshape(rows, half)
        pf_s[pl.ds(z, step)] = v.astype(BF).reshape(step, plane, half)
        fill(xpf, z + 1, step, v)

    each(grad_one)
    pf_halo = halo_copies(3, mid(xpf, 1), mid(xpf, depth))
    halo_start(pf_halo)
    wgrad(xr, pf_s, 0)
    f1 = level_1(0)
    parts["a2"].wait_send()
    parts["a1"].start()
    g3 = level_3(1, g2)
    halo_finish(pf_halo, 3, xpf)
    each(lambda z: put(igrad, z, 1, block(c_in, z, 1, 0) + conv(xpf, flat(wt, 0), z)))
    f2 = level_2(0, f1)
    parts["a2"].wait_recv()
    a_halo = halo_copies(
        4, a_in.at[0, 0, :, :, pl.ds(half, half)], a_in.at[0, depth - 1, :, :, pl.ds(half, half)]
    )
    halo_start(a_halo)
    each(lambda z: fill(xa, z + 1, step, block(a_in, z, 1, 0)))
    halo_finish(a_halo, 4, xa)

    def forward_conv(z):
        gz_s[pl.ds(z, step)] = jnp.tanh(conv(xa, flat(w, 0, 0), z)).reshape(step, plane, half)

    each(forward_conv)
    parts["a1"].wait()

    def forward_one(z):
        b1 = block(a_in, z, 0, 0) + gz_s[pl.ds(z, step)].reshape(rows, half)
        put(fwd, z, 0, b1)
        fill(xb, z + 1, step, b1)

    each(forward_one)
    b_halo = halo_copies(5, mid(xb, 1), mid(xb, depth))
    halo_start(b_halo)
    f3 = level_3(0, f2)
    g4 = level_4(1, g3)
    halo_finish(b_halo, 5, xb)
    each(
        lambda z: put(
            fwd, z, 1, block(a_in, z, 1, 0) + jnp.tanh(conv(xb, flat(w, 0, 1), z))
        )
    )

    def lay_out(g):
        per = nt // 8
        for share in range(nt):
            r, first = share // per, (share % per) * tp
            count = min(27 - first, tp)
            gsum[g, pl.ds(first, count), pl.ds(16 * r, 16)] = total[
                g, share // 2, share % 2, pl.ds(0, count)
            ]

    g4.wait()
    lay_out(1)
    level_4(0, f3).wait()
    lay_out(0)


def shards(carried_act, stored_out, cotangent, weights, momentum):
    ns, nt = lax.axis_size("section"), lax.axis_size("tile")
    _, depth, hy, wx, chans = stored_out.shape
    half = chans // 2
    per = nt // 8
    tp = -(-27 // per)
    m = nt // 2
    step = 1
    field = (depth + 2, hy + 2, wx, 3 * half)
    sems = 12 + 4 + 2 * (2 + 2 * (m - 1))
    vm = pltpu.VMEM
    cells = depth * hy * wx
    flops = 16 * cells * 27 * half * half
    fwd, igrad, gsum = pl.pallas_call(
        functools.partial(kernel, ns, nt, tp, step),
        out_shape=(
            jax.ShapeDtypeStruct((depth, hy, wx, chans), BF),
            jax.ShapeDtypeStruct((depth, hy, wx, chans), BF),
            jax.ShapeDtypeStruct((2, 27, half, half), BF),
        ),
        in_specs=[
            pl.BlockSpec(memory_space=pl.ANY),
            pl.BlockSpec(memory_space=vm),
            pl.BlockSpec(memory_space=pl.ANY),
            pl.BlockSpec(memory_space=vm),
        ],
        out_specs=[pl.BlockSpec(memory_space=vm)] * 3,
        scratch_shapes=[vm(field, BF)] * 6
        + [
            vm((6, 2, hy, wx, half), BF),
            vm((1, depth, hy, wx, chans), BF),
            vm((1, depth, hy, wx, chans), BF),
            vm((depth, hy * wx, half), F32),
            vm((depth, hy * wx, half), F32),
            vm((2, 27, half, half), BF),
            vm((depth, hy * wx, half), BF),
            vm((depth, hy * wx, half), BF),
            vm((2, m, 2, tp, 16, half), BF),
            vm((2, m, tp, 16, half), BF),
            vm((2, m, tp, 16, half), BF),
            vm((2, m - 1, tp, 16, half), BF),
            vm((2, m, 2, tp, 16, half), BF),
            pltpu.SemaphoreType.DMA((sems,)),
            pltpu.SemaphoreType.DMA((sems,)),
        ],
        compiler_params=pltpu.CompilerParams(
            collective_id=0, has_side_effects=True, vmem_limit_bytes=56 * 1024 * 1024
        ),
        cost_estimate=pl.CostEstimate(
            flops=flops, bytes_accessed=12 * 1024 * 1024, transcendentals=4 * cells * half
        ),
    )(carried_act, stored_out, cotangent, weights)
    count = depth * nt * hy * wx
    scale = grad_weight / jnp.sqrt(jnp.float32(count))
    new_momentum = momentum_decay * momentum + gsum[None].astype(F32) * scale
    return (fwd[None], igrad[None], new_momentum)


def solution(mesh):
    field = P("section", "tile", None, None, None)
    held = P("section", None, None, None, None)
    return jax.shard_map(
        shards,
        mesh=mesh,
        in_specs=(field, field, field, held, held),
        out_specs=(field, field, held),
        check_vma=False,
    )
```
